512 devices in a mesh: fsdp: 16 (over z_hi, y, core), chan: 32 (over z_lo, x).
Axes of the slice: x: 4, y: 4, z: 16 (z_hi: 2, z_lo: 8; z = z_hi * 8 + z_lo), core: 2. Of those that a mesh axis runs over, the one named last changes fastest.
Arguments:
- xs_in: bfloat16 [8192, 16384], P('fsdp', 'chan'), may hold values from -6 to 6
- gate_in: bfloat16 [8192, 16384], P('fsdp', 'chan'), may hold values from -110 to 110
- bc_in: bfloat16 [8192, 4096], P('fsdp', 'chan'), may hold values from -6 to 6
- dt_raw: float32 [8192, 256], P('fsdp', 'chan'), may hold values from -7.8 to 1.8
- x_tail: bfloat16 [32, 3, 16384], P('fsdp', None, 'chan'), may hold values from -6 to 6
- bc_tail: bfloat16 [32, 3, 4096], P('fsdp', None, 'chan'), may hold values from -6 to 6
- conv_x_w: float32 [4, 16384], P(None, 'chan'), may hold values from -3 to 3
- conv_x_b: float32 [16384], P('chan'), may hold values from -2 to 2
- conv_bc_w: float32 [4, 4096], P(None, 'chan'), may hold values from -3 to 3
- conv_bc_b: float32 [4096], P('chan'), may hold values from -2 to 2
- dt_bias: float32 [256], P('chan'), may hold values from -1 to 0.5
- a_log: float32 [256], P('chan'), may hold values from -1.9 to 1.6
- skip_d: float32 [256], P('chan'), may hold values from 0.5 to 1.5
- state_in: float32 [32, 256, 64, 256], P('fsdp', 'chan'), may hold values from -0.5 to 0.5
- norm_gain: float32 [16384], P('chan'), may hold values from 0.1 to 1.9
- out_values: bfloat16 [16384, 4096], P('chan', 'fsdp'), may hold values from -0.09375 to 0.09375
- out_scales: float32 [128, 32], P('chan', 'fsdp'), may hold values from 0.5 to 2
Outputs:
- mixed_out: bfloat16 [8192, 4096], P('fsdp', 'chan')
- new_state: float32 [32, 256, 64, 256], P('fsdp', 'chan')
The draws below stay inside these ranges and needn't reach their ends.
All inputs are finite; a program needn't handle non-finite values.
Results may differ from the reference program's by a relative error of at most 0.03.
Values may be sent and summed in bfloat16 or wider, within the bound.
A program may use at most 64 MiB of HBM per device.

```python
import math
import jax
import jax.numpy as jnp
from jax import lax

D = 4096
HEAD_P = 64
STATE = 256
CONV = 4
BLOCK = 128
SPAN = 256
MIXER_HEADS = 256
GROUPS = 8
INNER = 16384
REQS = 32
TOTAL_TOKENS = 8192
N_CHAN = 32


def draw_dt_raw(key, part):
    key = jax.random.fold_in(key, 11)
    base_key, place_key, magnitude_key = jax.random.split(key, 3)
    reference_level = -5.0 + 0.7 * jnp.clip(jax.random.normal(base_key, (TOTAL_TOKENS, MIXER_HEADS), jnp.float32), -4.0, 4.0)
    positions_chosen = jax.random.randint(place_key, (REQS, 3), 0, SPAN) + SPAN * jnp.arange(REQS, dtype=jnp.int32)[:, None]
    spike_rows = jnp.any(jnp.arange(TOTAL_TOKENS, dtype=jnp.int32)[:, None] == positions_chosen.reshape(1, -1), axis=1)
    spike_magnitude = jax.random.uniform(magnitude_key, (TOTAL_TOKENS, MIXER_HEADS), jnp.float32, 1.0, 1.8)
    return jnp.where(spike_rows[:, None], spike_magnitude, reference_level)


def draw_a_log(key, part):
    key = jax.random.fold_in(key, 23)
    return jax.random.uniform(key, (MIXER_HEADS,), jnp.float32, -1.9, 1.6)


def scaled_gate(key, rise, normals):
    row_key, col_key = jax.random.split(key, 2)
    row_scale = 0.3 * jnp.exp(jax.random.uniform(row_key, (TOTAL_TOKENS, 1), jnp.float32, 0.0, math.log(10.0)))
    col_scale = 0.3 * jnp.exp(jax.random.uniform(col_key, (1, INNER), jnp.float32, 0.0, math.log(10.0)))
    group_cols = INNER // GROUPS
    position = (jnp.arange(INNER, dtype=jnp.int32) % group_cols).astype(jnp.float32) / group_cols
    return normals * row_scale * col_scale * jnp.exp(position * math.log(rise))[None, :]


def draw_gate_in(key, part):
    key = jax.random.fold_in(key, 37)
    noise_key, scale_key = jax.random.split(key, 2)
    normals = jnp.clip(jax.random.normal(noise_key, (TOTAL_TOKENS, INNER), jnp.float32), -4.0, 4.0)
    return scaled_gate(scale_key, 3.0, normals).astype(jnp.bfloat16)


def raised(drawn, own_key, source, target, blocks, factor):
    owner, partner = [(jnp.arange(drawn.shape[axis_at]) // (drawn.shape[axis_at] // blocks)).reshape([-1 if axis == axis_at else 1 for axis in range(drawn.ndim)]) for axis_at in (source, target)]
    chosen = jax.random.permutation(own_key, blocks)[partner]
    strong = (owner == chosen) | (owner == (partner + blocks // 2) % blocks)
    return jnp.where(strong, factor * drawn, drawn)


def block_scale(rng, shape, cuts, smallest, high):
    def one(dim, parts):
        draws = jax.random.uniform(jax.random.fold_in(jax.random.fold_in(rng, 6), dim), (parts,), jnp.float32, smallest / len(cuts), high / len(cuts))
        return jnp.repeat(jnp.exp(draws), shape[dim] // parts).reshape((-1,) + (1,) * (len(shape) - dim - 1))

    level = one(*cuts[0])
    for cut in cuts[1:]:
        level = level * one(*cut)
    return level


def bell_draw(rng, extent, scale, reach, pieces=(), held_as=jnp.bfloat16):
    drawn = scale * jax.random.normal(rng, extent, jnp.float32)
    if pieces:
        drawn = drawn * block_scale(rng, extent, pieces, -0.22, 0.18)
    return jnp.clip(drawn, -reach, reach).astype(held_as)


def heavy_noise(rng, dims, scale, most, pieces, heavy, held_as=jnp.bfloat16):
    entries = scale * jax.random.normal(rng, dims, jnp.float32)
    if pieces:
        entries = entries * block_scale(rng, dims, pieces, -0.22, 0.18)
    return jnp.clip(raised(entries, jax.random.fold_in(rng, 3), *heavy), -most, most).astype(held_as)


def setup_inputs(seed: int = 0) -> dict:
    key_list = jax.random.split(jax.random.key(seed), 18)
    return {
        "xs_in": bell_draw(key_list[0], (TOTAL_TOKENS, INNER), 1.0, 6.0, ((0, 16), (1, 32))),
        "gate_in": draw_gate_in(jax.random.fold_in(key_list[17], 71), 0),
        "bc_in": bell_draw(key_list[2], (TOTAL_TOKENS, GROUPS * 2 * STATE), 1.0, 6.0, ((0, 16), (1, 32))),
        "dt_raw": draw_dt_raw(jax.random.fold_in(key_list[17], 71), 0),
        "x_tail": bell_draw(key_list[4], (REQS, CONV - 1, INNER), 1.0, 6.0, ((0, 16), (2, 32))),
        "bc_tail": bell_draw(key_list[5], (REQS, CONV - 1, GROUPS * 2 * STATE), 1.0, 6.0, ((0, 16), (2, 32))),
        "conv_x_w": bell_draw(key_list[6], (CONV, INNER), CONV ** -0.5, 3.0, ((1, 32),), jnp.float32),
        "conv_x_b": bell_draw(key_list[7], (INNER,), 0.5, 2.0, ((0, 32),), jnp.float32),
        "conv_bc_w": bell_draw(key_list[8], (CONV, GROUPS * 2 * STATE), CONV ** -0.5, 3.0, ((1, 32),), jnp.float32),
        "conv_bc_b": bell_draw(key_list[9], (GROUPS * 2 * STATE,), 0.5, 2.0, ((0, 32),), jnp.float32),
        "dt_bias": jnp.clip(-1.0 + 1.5 * jax.random.uniform(key_list[10], (MIXER_HEADS,), jnp.float32) ** block_scale(key_list[10], (MIXER_HEADS,), ((0, 32),), -0.2, 0.2), -1.0, 0.5),
        "a_log": draw_a_log(jax.random.fold_in(key_list[17], 71), 0),
        "skip_d": jnp.clip(0.5 + 1.0 * jax.random.uniform(key_list[12], (MIXER_HEADS,), jnp.float32) ** block_scale(key_list[12], (MIXER_HEADS,), ((0, 32),), -0.2, 0.2), 0.5, 1.5),
        "state_in": bell_draw(key_list[13], (REQS, MIXER_HEADS, HEAD_P, STATE), 0.0625, 0.5, ((0, 16), (1, 32)), jnp.float32),
        "norm_gain": jnp.clip(1.0 + 0.18 * jax.random.normal(key_list[14], (INNER,), jnp.float32), 0.1, 1.9),
        "out_values": heavy_noise(key_list[15], (INNER, D), INNER ** -0.5, 0.09375, ((0, 32), (1, 16)), (0, 1, 32, 2.75)),
        "out_scales": jnp.clip(jnp.exp(math.log(2.0) - 1.3862944 * jax.random.uniform(key_list[16], (INNER // BLOCK, D // BLOCK), jnp.float32) ** block_scale(key_list[16], (INNER // BLOCK, D // BLOCK), ((0, 32), (1, 16)), -0.2, 0.2)), 0.5, 2.0),
    }


EPS = 1e-05

def causal_conv(inputs, prefix, weight, offset):
    padded = jnp.concatenate([prefix, inputs], axis=1).astype(jnp.float32)
    length = inputs.shape[1]
    tap_count = weight.shape[0]
    running = offset[None, None, :] + weight[0][None, None, :] * padded[:, 0:length]
    for tap_index in range(1, tap_count):
        running = running + weight[tap_index][None, None, :] * padded[:, tap_index:tap_index + length]
    return jax.nn.silu(running).astype(jnp.bfloat16)

def span_scan(x_heads, b_state, c_state, step_size, decay_rate, skip_gain, carried):
    length = step_size.shape[0]
    highest = lax.Precision.HIGHEST
    scores = jnp.dot(c_state.astype(jnp.float32), b_state.astype(jnp.float32).T, precision=highest)
    log_decay = jnp.cumsum(-decay_rate[None, :] * step_size, axis=0)
    by_head = log_decay.T
    spread = by_head[:, :, None] - by_head[:, None, :]
    row_ids = lax.broadcasted_iota(jnp.int32, (length, length), 0)
    col_ids = lax.broadcasted_iota(jnp.int32, (length, length), 1)
    causal = (row_ids >= col_ids)[None]
    decay = jnp.where(causal, jnp.exp(jnp.where(causal, spread, 0.0)), 0.0)
    mixing = (scores[None] * decay * step_size.T[:, None, :]).astype(jnp.bfloat16)
    within = jnp.einsum('hts,shp->thp', mixing.astype(jnp.float32), x_heads.astype(jnp.float32), precision=highest)
    from_state = jnp.einsum('tn,hpn->thp', c_state.astype(jnp.float32), carried, precision=highest)
    from_state = from_state * jnp.exp(log_decay)[:, :, None]
    outputs = within + from_state + skip_gain[None, :, None] * x_heads.astype(jnp.float32)
    final_log = log_decay[-1]
    weighting = jnp.exp(final_log[None, :] - log_decay) * step_size
    weighted = x_heads.astype(jnp.float32) * weighting[:, :, None]
    updated = jnp.exp(final_log)[:, None, None] * carried + jnp.einsum('shp,sn->hpn', weighted, b_state.astype(jnp.float32), precision=highest)
    return (outputs, updated)

def reference(xs_in, gate_in, bc_in, dt_raw, x_tail, bc_tail, conv_x_w, conv_x_b, conv_bc_w, conv_bc_b, dt_bias, a_log, skip_d, state_in, norm_gain, out_values, out_scales):
    request_count = state_in.shape[0]
    length = xs_in.shape[0] // request_count
    head_count = dt_raw.shape[1]
    head_width = state_in.shape[2]
    state_width = state_in.shape[3]
    groups = bc_in.shape[1] // (2 * state_width)
    per_group = head_count // groups
    inner = head_count * head_width
    group_cols = inner // groups
    step_size = jax.nn.softplus(dt_raw + dt_bias[None, :]).reshape(request_count, length, head_count)
    decay_rate = jnp.exp(a_log)

    def one_request(request_args):
        x_rows, z_rows, bc_rows, x_prefix, bc_prefix, step_rows, carried = request_args
        x_conv = causal_conv(x_rows[None], x_prefix[None], conv_x_w, conv_x_b)[0]
        bc_conv = causal_conv(bc_rows[None], bc_prefix[None], conv_bc_w, conv_bc_b)[0]
        x_grouped = x_conv.reshape(length, groups, per_group, head_width).transpose(1, 0, 2, 3)
        bc_grouped = bc_conv.reshape(length, groups, 2 * state_width).transpose(1, 0, 2)
        step_grouped = step_rows.reshape(length, groups, per_group).transpose(1, 0, 2)

        def one_group(group_args):
            x_heads, bc_group, step_group, rate_group, skip_group, carried_group = group_args
            return span_scan(x_heads, bc_group[:, :state_width], bc_group[:, state_width:], step_group, rate_group, skip_group, carried_group)
        outputs, updated = lax.map(one_group, (x_grouped, bc_grouped, step_grouped, decay_rate.reshape(groups, per_group), skip_d.reshape(groups, per_group), carried.reshape(groups, per_group, head_width, state_width)))
        ssd_rows = outputs.transpose(1, 0, 2, 3).reshape(length, inner)
        gated = ssd_rows * jax.nn.silu(z_rows.astype(jnp.float32))
        grouped = gated.reshape(length, groups, group_cols)
        mean_sq = lax.optimization_barrier(jnp.mean(grouped * grouped, axis=2, keepdims=True))
        normed = (grouped * lax.rsqrt(mean_sq + EPS)).reshape(length, inner) * norm_gain[None, :]
        return (normed.astype(jnp.bfloat16), updated.reshape(head_count, head_width, state_width))
    hidden, new_state = lax.map(one_request, (xs_in.reshape(request_count, length, inner), gate_in.reshape(request_count, length, inner), bc_in.reshape(request_count, length, -1), x_tail, bc_tail, step_size, state_in))
    hidden = hidden.reshape(request_count * length, inner)
    scales = jnp.repeat(jnp.repeat(out_scales, BLOCK, axis=0), BLOCK, axis=1)
    weight_eff = (out_values.astype(jnp.float32) * scales).astype(jnp.bfloat16)
    inner_dev = inner // N_CHAN
    token_rows = request_count * length
    out_cols = out_values.shape[1]

    def add_block(block_index, running):
        first = (block_index * inner_dev).astype(jnp.int32)
        hidden_block = lax.dynamic_slice_in_dim(hidden, first, inner_dev, 1).astype(jnp.float32)
        weight_block = lax.dynamic_slice_in_dim(weight_eff, first, inner_dev, 0).astype(jnp.float32)
        block_term = jnp.dot(hidden_block, weight_block, precision=lax.Precision.HIGHEST).astype(jnp.bfloat16)
        block_term = lax.optimization_barrier(block_term)
        return running + block_term.astype(jnp.float32)
    mixed_out = lax.fori_loop(0, N_CHAN, add_block, jnp.zeros((token_rows, out_cols), jnp.float32))
    return (mixed_out.astype(jnp.bfloat16), new_state)
```

```python
import functools

import jax
import jax.numpy as jnp
from jax import lax
from jax.experimental import pallas as pl
from jax.experimental.pallas import tpu as pltpu
from jax.sharding import PartitionSpec as P

EPS = 1e-05
MESH = pl.DeviceIdType.MESH
F32 = jnp.float32
BF16 = jnp.bfloat16
NEG = -1e30
HIGHEST = lax.Precision.HIGHEST


def silu(v):
    return v / (1.0 + jnp.exp(-v))


def dot_nt(a, b):
    return lax.dot_general(a, b, (((1,), (1,)), ((), ())), preferred_element_type=F32)


def dot_tn(a, b):
    return lax.dot_general(a, b, (((0,), (0,)), ((), ())), preferred_element_type=F32)


def dot_nn(a, b):
    return jnp.dot(a, b, preferred_element_type=F32)


def kernel(
    xs, gate, bc, dt, x_tail, bc_tail, cxw, cxb, cbw, cbb, dt_bias, a_log, skip_d, state, gain,
    values, scales,
    out, new_state,
    wsrc, wfull, bcall, gall, xact, conv_x, conv_b, ldc, stc, ldr, stp, score, part, sbuf, rbuf,
    a2a_send, a2a_recv, y_send, z_send, w_recv, sib_send, sib_recv, bc_send, bc_recv,
    g_send, g_recv, s_send, s_recv,
):
    f = lax.axis_index("fsdp")
    ch = lax.axis_index("chan")
    zh, y, c = lax.div(f, 8), lax.rem(lax.div(f, 2), 4), lax.rem(f, 2)
    zl, x = lax.div(ch, 4), lax.rem(ch, 4)
    x_owner = lax.div(x, 2)
    d_me = zh * 4 + y
    d_far = (1 - zh) * 4 + y

    def at(zh=zh, y=y, c=c, zl=zl, x=x):
        return ((zh * 4 + y) * 2 + c, zl * 4 + x)

    def xn(j, core=c):
        return at(x=lax.rem(x + j, 4), c=core)

    def yn(j):
        return at(y=lax.rem(y + j, 4))

    def zn(step):
        z = lax.rem(zh * 8 + zl + step, 16)
        return at(zh=lax.div(z, 8), zl=lax.rem(z, 8))

    sibling = at(c=1 - c)
    opposite = at(zh=1 - zh)

    def rcopy(src, dst, send, recv, device):
        return pltpu.make_async_remote_copy(
            src_ref=src, dst_ref=dst, send_sem=send, recv_sem=recv, device_id=device,
            device_id_type=MESH,
        )

    bar = pltpu.get_barrier_semaphore()
    others = [xn(j, core) for j in (1, 2, 3) for core in (c, 1 - c)]
    others += [yn(j) for j in (1, 2, 3)] + [zn(1), zn(15), opposite, sibling]
    for device in others:
        pl.semaphore_signal(bar, inc=1, device_id=device, device_id_type=MESH)
    gain_rows = jnp.transpose(jnp.broadcast_to(gain[...], (128, 512)))
    for k in range(4):
        for b in range(2):
            tile = values[k * 128:(k + 1) * 128, b * 128:(b + 1) * 128].astype(F32)
            tile = tile * scales[k, b] * gain_rows[k * 128:(k + 1) * 128]
            wsrc[b, k] = tile.astype(BF16)
    pl.semaphore_wait(bar, len(others))

    def a2a(b, q):
        return rcopy(
            wsrc.at[b, pl.ds(2 * q, 2)], wfull.at[d_me, pl.ds(2 * q, 2), x],
            a2a_send.at[b, q], a2a_recv.at[x], at(x=2 * c + b, c=q),
        )

    def a2a_local(b, q):
        return jnp.logical_and(x == 2 * c + b, c == q)

    for b in range(2):
        for q in range(2):
            @pl.when(jnp.logical_not(a2a_local(b, q)))
            def _():
                a2a(b, q).start()

            @pl.when(a2a_local(b, q))
            def _():
                wfull[d_me, 2 * q, x] = wsrc[b, 2 * q]
                wfull[d_me, 2 * q + 1, x] = wsrc[b, 2 * q + 1]

    def conv(scratch, rows, tail, w, b, lanes):
        scratch[5:8, lanes] = tail.astype(F32)
        scratch[8:264, lanes] = rows.astype(F32)
        total = b[:, lanes]
        for k in range(4):
            total = total + w[k:k + 1, lanes] * scratch[5 + k:261 + k, lanes]
        return silu(total).astype(BF16)

    def bc_copy(r, j):
        return rcopy(
            bcall.at[x, r], bcall.at[x, r], bc_send.at[r, j - 1], bc_recv.at[x, r], xn(j)
        )

    for r in range(2):
        bcall[x, r] = conv(conv_b, bc[r], bc_tail[r], cbw, cbb, slice(0, 128))
        for j in (1, 3, 2):
            bc_copy(r, j).start()

    row = lax.broadcasted_iota(jnp.int32, (256, 256), 0)
    col = lax.broadcasted_iota(jnp.int32, (256, 256), 1)
    tril = (row >= col).astype(F32)
    rate = jnp.exp(a_log[...])

    def prepare(r):
        v = dt[r] + dt_bias[...]
        step = jnp.maximum(v, 0.0) + jnp.log1p(jnp.exp(-jnp.abs(v)))
        ldc[r] = jnp.zeros((256, 128), F32)
        stc[r] = jnp.zeros((256, 128), F32)
        ldc[r, :, 0:8] = jnp.dot(
            tril, -rate * step, precision=HIGHEST, preferred_element_type=F32
        )
        stc[r, :, 0:8] = step
        ldr[r] = jnp.transpose(ldc[r])[0:8]
        stp[r] = jnp.transpose(stc[r])[0:8]
        for p in range(4):
            lanes = slice(p * 128, (p + 1) * 128)
            xact[r, p] = conv(conv_x, xs[r, :, lanes], x_tail[r, :, lanes], cxw, cxb, lanes)

    lane = lax.broadcasted_iota(jnp.int32, (1, 128), 1)
    low = lane < 64
    r128 = lax.broadcasted_iota(jnp.int32, (128, 128), 0)
    c128 = lax.broadcasted_iota(jnp.int32, (128, 128), 1)
    upper = jnp.where(r128 >= c128, 0.0, NEG)

    def pick(table, r, p, rows=slice(None)):
        return jnp.where(
            low, table[r, rows, 2 * p:2 * p + 1], table[r, rows, 2 * p + 1:2 * p + 2]
        )

    def b_rows(r):
        return jnp.concatenate([bcall[0, r], bcall[1, r]], axis=1)

    def ssd(r):
        c_rows = jnp.concatenate([bcall[2, r], bcall[3, r]], axis=1)
        score[...] = dot_nt(c_rows, b_rows(r))
        for p in range(4):
            lanes = slice(p * 128, (p + 1) * 128)
            xp = xact[r, p]
            masked = [jnp.where(low, xp, 0).astype(BF16), jnp.where(low, 0, xp).astype(BF16)]
            top, bottom = [], []
            for e in range(2):
                h = 2 * p + e

                def mix(i, j):
                    ri, rj = slice(i * 128, i * 128 + 128), slice(j * 128, j * 128 + 128)
                    spread = ldc[r, ri, h:h + 1] - ldr[r, h:h + 1, rj]
                    if i == j:
                        spread = spread + upper
                        spread = jnp.minimum(spread, 0.0)
                    return (score[ri, rj] * jnp.exp(spread) * stp[r, h:h + 1, rj]).astype(BF16)

                top.append(mix(0, 0))
                bottom += [mix(1, 0), mix(1, 1)]
            y_top = dot_nn(
                jnp.concatenate(top, axis=1),
                jnp.concatenate([masked[0][:128], masked[1][:128]], axis=0),
            )
            y_bottom = dot_nn(
                jnp.concatenate(bottom, axis=1), jnp.concatenate(masked, axis=0)
            )
            held = state[r, 2 * p:2 * p + 2].reshape(128, 256).astype(BF16)
            from_state = dot_nt(c_rows, held)
            skip = jnp.where(low, skip_d[0, 2 * p], skip_d[0, 2 * p + 1])
            rows = jnp.concatenate([y_top, y_bottom], axis=0)
            rows = rows + from_state * jnp.exp(pick(ldc, r, p)) + skip * xp.astype(F32)
            gall[r, x, p] = (rows * silu(gate[r, :, lanes].astype(F32))).astype(BF16)

    def carry(r):
        for p in range(4):
            last = pick(ldc, r, p, slice(255, 256))
            weight = jnp.exp(last - pick(ldc, r, p)) * pick(stc, r, p)
            xw = (xact[r, p].astype(F32) * weight).astype(BF16)
            update = dot_tn(xw, b_rows(r))
            for e in range(2):
                h = 2 * p + e
                decay = jnp.exp(ldc[r, 255:256, h:h + 1])
                new_state[r, h] = decay * state[r, h] + update[e * 64:(e + 1) * 64]

    def y_copy(half, d, s, j):
        piece = wfull.at[d, 2 * c + s]
        return rcopy(piece, piece, y_send.at[half, s, j - 1], w_recv.at[d, s], yn(j))

    def z_copy(s):
        piece = wfull.at[d_me, 2 * c + s]
        return rcopy(piece, piece, z_send.at[s], w_recv.at[d_me, s], opposite)

    def sib_copy(d, s):
        piece = wfull.at[d, 2 * c + s]
        return rcopy(piece, piece, sib_send.at[d, s], sib_recv.at[d, s], sibling)

    def w_wait(d, s):
        piece = wfull.at[d, 2 * c + s]
        rcopy(piece, piece, z_send.at[s], w_recv.at[d, s], opposite).wait_recv()

    def sib_wait(d, s):
        piece = wfull.at[d, 2 * (1 - c) + s]
        rcopy(piece, piece, sib_send.at[d, s], sib_recv.at[d, s], sibling).wait_recv()

    def spread_own():
        for j in range(4):
            @pl.when(jnp.logical_not(jnp.logical_and(x == j, c == x_owner)))
            def _():
                rcopy(
                    wsrc.at[0, pl.ds(0, 2)], wfull.at[d_me, pl.ds(2 * c, 2), j],
                    a2a_send.at[0, 0], a2a_recv.at[j], sibling,
                ).wait_recv()

        for s in range(2):
            z_copy(s).start()
        for s in range(2):
            for j in (1, 3, 2):
                y_copy(0, d_me, s, j).start()
            sib_copy(d_me, s).start()

    def spread_far(s):
        w_wait(d_far, s)
        for j in (1, 3, 2):
            y_copy(1, d_far, s, j).start()
        sib_copy(d_far, s).start()

    def hand_over(half, s):
        for j in (1, 3, 2):
            d = half * 4 + lax.rem(y + j, 4)
            w_wait(d, s)
            sib_copy(d, s).start()

    def sib_all(half):
        for i in range(4):
            for s in range(2):
                sib_wait(half * 4 + i, s)

    def g_copy(r, j):
        return rcopy(gall.at[r, x], gall.at[r, x], g_send.at[r, j - 1], g_recv.at[r, x], xn(j))

    def g_start(r):
        for j in (1, 3, 2):
            g_copy(r, j).start()

    def g_wait(r):
        for j in (1, 3, 2):
            source = lax.rem(x + j, 4)
            slot = gall.at[r, source]
            rcopy(slot, slot, g_send.at[r, j - 1], g_recv.at[r, source], xn(j)).wait_recv()

    def bc_wait(r):
        for j in (1, 3, 2):
            source = lax.rem(x + j, 4)
            slot = bcall.at[source, r]
            rcopy(slot, slot, bc_send.at[r, j - 1], bc_recv.at[source, r], xn(j)).wait_recv()

    def row_factor(r):
        total = jnp.zeros((256, 128), F32)
        for k in range(4):
            for j in range(4):
                block = gall[r, j, k].astype(F32)
                total = total + block * block
        return lax.rsqrt(jnp.sum(total, axis=1, keepdims=True) / 2048.0 + EPS)

    def project(r, half):
        factor = row_factor(r)
        rows = jnp.concatenate([gall[r, j, k] for k in range(4) for j in range(4)], axis=1)
        for i in range(2):
            d = half * 4 + 2 * i
            both = jnp.concatenate(
                [wfull[d].reshape(2048, 128), wfull[d + 1].reshape(2048, 128)], axis=1
            )
            product = dot_nn(rows, both) * factor
            part[r, d] = product[:, :128]
            part[r, d + 1] = product[:, 128:]

    def s_copy(r, d, way):
        target = at(zl=zl + 1 - 2 * way)
        return rcopy(
            sbuf.at[r, d], rbuf.at[way, r, d], s_send.at[r, d], s_recv.at[way, r, d], target
        )

    def s_wait(r, d, way):
        slot = rbuf.at[way, r, d]
        rcopy(slot, slot, s_send.at[r, d], s_recv.at[way, r, d], sibling).wait_recv()

    def order(half, i):
        seat = zl + half * (7 - 2 * zl)
        near = jnp.maximum(3 - seat, 0)
        d = jnp.where(i < near, 3 - i, i - near)
        inside = seat < 4
        return d + half * (7 - 2 * d), near, inside

    def relay(r, d):
        way = (d < zl).astype(jnp.int32)
        fed = (zl + way * (7 - 2 * zl)) > 0

        @pl.when(fed)
        def _():
            s_wait(r, d, way)
            sbuf[r, d] = (part[r, d] + rbuf[way, r, d].astype(F32)).astype(BF16)

        @pl.when(jnp.logical_not(fed))
        def _():
            sbuf[r, d] = part[r, d].astype(BF16)

        s_copy(r, d, way).start()

    def relay_near(r, half):
        def body(i, carry_):
            d, near, inside = order(half, i)

            @pl.when(jnp.logical_or(jnp.logical_not(inside), i < near))
            def _():
                relay(r, d)

            return carry_

        lax.fori_loop(0, 4, body, 0)

    def relay_far(r, half):
        def body(i, carry_):
            d, near, inside = order(half, i)

            @pl.when(jnp.logical_and(inside, i >= near))
            def _():
                relay(r, d)

            return carry_

        lax.fori_loop(0, 3, body, 0)

    def finish(r):
        @pl.when(zl > 0)
        def _():
            s_wait(r, zl, 0)
            part[r, zl] = part[r, zl] + rbuf[0, r, zl].astype(F32)

        @pl.when(zl < 7)
        def _():
            s_wait(r, zl, 1)
            part[r, zl] = part[r, zl] + rbuf[1, r, zl].astype(F32)

        out[r] = part[r, zl].astype(BF16)

    prepare(0)
    spread_own()
    prepare(1)
    bc_wait(0)
    ssd(0)
    g_start(0)
    bc_wait(1)
    ssd(1)
    g_start(1)
    for s in range(2):
        hand_over(zh, s)
    carry(0)
    carry(1)
    spread_far(0)
    sib_all(zh)
    g_wait(0)
    project(0, zh)
    relay_near(0, zh)
    g_wait(1)
    project(1, zh)
    relay_near(1, zh)
    hand_over(1 - zh, 0)
    spread_far(1)
    relay_far(0, zh)
    relay_far(1, zh)
    hand_over(1 - zh, 1)
    sib_all(1 - zh)
    project(0, 1 - zh)
    relay_near(0, 1 - zh)
    project(1, 1 - zh)
    relay_near(1, 1 - zh)
    relay_far(0, 1 - zh)
    relay_far(1, 1 - zh)
    finish(0)
    finish(1)

    for b in range(2):
        for q in range(2):
            @pl.when(jnp.logical_not(a2a_local(b, q)))
            def _():
                a2a(b, q).wait_send()
    for s in range(2):
        z_copy(s).wait_send()
        for j in (1, 2, 3):
            y_copy(0, d_me, s, j).wait_send()
            y_copy(1, d_far, s, j).wait_send()
        for d in range(8):
            sib_copy(d, s).wait_send()
    for r in range(2):
        for j in (1, 2, 3):
            bc_copy(r, j).wait_send()
            g_copy(r, j).wait_send()
        for d in range(8):
            @pl.when(d != zl)
            def _():
                s_copy(r, d, (d < zl).astype(jnp.int32)).wait_send()


def per_device(
    xs_in, gate_in, bc_in, dt_raw, x_tail, bc_tail, conv_x_w, conv_x_b, conv_bc_w, conv_bc_b,
    dt_bias, a_log, skip_d, state_in, norm_gain, out_values, out_scales,
):
    vmem = pl.BlockSpec(memory_space=pltpu.VMEM)
    smem = pl.BlockSpec(memory_space=pltpu.SMEM)
    dma = pltpu.SemaphoreType.DMA
    out, new_state = pl.pallas_call(
        kernel,
        name="mixer",
        out_shape=(
            jax.ShapeDtypeStruct((2, 256, 128), BF16),
            jax.ShapeDtypeStruct(state_in.shape, F32),
        ),
        in_specs=[vmem] * 12 + [smem] + [vmem] * 3 + [smem],
        out_specs=(vmem, vmem),
        scratch_shapes=[
            pltpu.VMEM((2, 4, 128, 128), BF16),
            pltpu.VMEM((8, 4, 4, 128, 128), BF16),
            pltpu.VMEM((4, 2, 256, 128), BF16),
            pltpu.VMEM((2, 4, 4, 256, 128), BF16),
            pltpu.VMEM((2, 4, 256, 128), BF16),
            pltpu.VMEM((264, 512), F32),
            pltpu.VMEM((264, 128), F32),
            pltpu.VMEM((2, 256, 128), F32),
            pltpu.VMEM((2, 256, 128), F32),
            pltpu.VMEM((2, 8, 256), F32),
            pltpu.VMEM((2, 8, 256), F32),
            pltpu.VMEM((256, 256), F32),
            pltpu.VMEM((2, 8, 256, 128), F32),
            pltpu.VMEM((2, 8, 256, 128), BF16),
            pltpu.VMEM((2, 2, 8, 256, 128), BF16),
            dma((2, 2)),
            dma((4,)),
            dma((2, 2, 3)),
            dma((2,)),
            dma((8, 2)),
            dma((8, 2)),
            dma((8, 2)),
            dma((2, 3)),
            dma((4, 2)),
            dma((2, 3)),
            dma((2, 4)),
            dma((2, 8)),
            dma((2, 2, 8)),
        ],
        compiler_params=pltpu.CompilerParams(
            collective_id=0, has_side_effects=True, vmem_limit_bytes=44 * 1024 * 1024
        ),
    )(
        xs_in.reshape(2, 256, 512), gate_in.reshape(2, 256, 512), bc_in.reshape(2, 256, 128),
        dt_raw.reshape(2, 256, 8), x_tail, bc_tail, conv_x_w, conv_x_b.reshape(1, 512),
        conv_bc_w, conv_bc_b.reshape(1, 128), dt_bias.reshape(1, 8), a_log.reshape(1, 8),
        skip_d.reshape(1, 8), state_in, norm_gain.reshape(1, 512), out_values, out_scales,
    )
    return out.reshape(512, 128), new_state


def solution(mesh):
    placed = (
        P("fsdp", "chan"),
        P("fsdp", "chan"),
        P("fsdp", "chan"),
        P("fsdp", "chan"),
        P("fsdp", None, "chan"),
        P("fsdp", None, "chan"),
        P(None, "chan"),
        P("chan"),
        P(None, "chan"),
        P("chan"),
        P("chan"),
        P("chan"),
        P("chan"),
        P("fsdp", "chan", None, None),
        P("chan"),
        P("chan", "fsdp"),
        P("chan", "fsdp"),
    )
    return jax.shard_map(
        per_device,
        mesh=mesh,
        in_specs=placed,
        out_specs=(P("fsdp", "chan"), P("fsdp", "chan", None, None)),
        check_vma=False,
    )
```

```python
import functools

import jax
import jax.numpy as jnp
from jax import lax
from jax.experimental import pallas as pl
from jax.experimental.pallas import tpu as pltpu
from jax.sharding import PartitionSpec as P

EPS = 1e-05
MESH = pl.DeviceIdType.MESH
F32 = jnp.float32
BF16 = jnp.bfloat16
NEG = -1e30
HIGHEST = lax.Precision.HIGHEST


def silu(v):
    return v / (1.0 + jnp.exp(-v))


def dot_nt(a, b):
    return lax.dot_general(a, b, (((1,), (1,)), ((), ())), preferred_element_type=F32)


def dot_tn(a, b):
    return lax.dot_general(a, b, (((0,), (0,)), ((), ())), preferred_element_type=F32)


def dot_nn(a, b):
    return jnp.dot(a, b, preferred_element_type=F32)


def kernel(*refs):
    hbm, (out, state_out), held, refs = refs[:17], refs[17:19], refs[19:36], refs[36:]
    (
        xs, gate, bc, dt, x_tail, bc_tail, cxw, cxb, cbw, cbb, dt_bias, a_log, skip_d, state, gain,
        values, scales,
    ) = held
    (
        wsrc, wfull, bcall, gall, xact, conv_x, conv_b, ldc, stc, ldr, stp, score, part, sbuf,
        rbuf, new_state, in_sem, out_sem, a2a_send, a2a_recv, y_send, z_send, w_recv, sib_send, sib_recv, bc_send,
        bc_recv, g_send, g_recv, s_send, s_recv,
    ) = refs
    f = lax.axis_index("fsdp")
    ch = lax.axis_index("chan")
    zh, y, c = lax.div(f, 8), lax.rem(lax.div(f, 2), 4), lax.rem(f, 2)
    zl, x = lax.div(ch, 4), lax.rem(ch, 4)
    x_owner = lax.div(x, 2)
    d_me = zh * 4 + y
    d_far = (1 - zh) * 4 + y

    def at(zh=zh, y=y, c=c, zl=zl, x=x):
        return ((zh * 4 + y) * 2 + c, zl * 4 + x)

    def xn(j, core=c):
        return at(x=lax.rem(x + j, 4), c=core)

    def yn(j):
        return at(y=lax.rem(y + j, 4))

    def zn(step):
        z = lax.rem(zh * 8 + zl + step, 16)
        return at(zh=lax.div(z, 8), zl=lax.rem(z, 8))

    sibling = at(c=1 - c)
    opposite = at(zh=1 - zh)

    def rcopy(src, dst, send, recv, device):
        return pltpu.make_async_remote_copy(
            src_ref=src, dst_ref=dst, send_sem=send, recv_sem=recv, device_id=device,
            device_id_type=MESH,
        )

    bar = pltpu.get_barrier_semaphore()
    half_line, seat_line = lax.div(zl, 4), lax.rem(zl, 4)
    depth = seat_line + half_line * (3 - 2 * seat_line)
    others = [xn(j, core) for j in (1, 2, 3) for core in (c, 1 - c)]
    others += [yn(j) for j in (1, 2, 3)] + [zn(1), zn(15), opposite, sibling]
    for device in others + [at(zl=4 - half_line)]:
        pl.semaphore_signal(bar, inc=1, device_id=device, device_id_type=MESH)

    def fetch(i):
        return pltpu.make_async_copy(hbm[i], held[i], in_sem.at[i])

    for i in (15, 14, 16, 2, 5, 8, 9, 3, 10, 11, 0, 4, 6, 7, 13, 1, 12):
        fetch(i).start()

    for i in (15, 14, 16):
        fetch(i).wait()
    gain_rows = jnp.transpose(jnp.broadcast_to(gain[...], (128, 512)))
    for k in range(4):
        for b in range(2):
            tile = values[k * 128:(k + 1) * 128, b * 128:(b + 1) * 128].astype(F32)
            tile = tile * scales[b:b + 1, k:k + 1] * gain_rows[k * 128:(k + 1) * 128]
            wsrc[b, k] = tile.astype(BF16)

    def conv(scratch, rows, tails, r, w, b, lanes):
        for k in range(3):
            scratch[5 + k:6 + k, lanes] = tails[k].astype(F32)[r:r + 1, lanes]
        scratch[8:264, lanes] = rows.astype(F32)
        total = b[:, lanes]
        for k in range(4):
            total = total + w[k:k + 1, lanes] * scratch[5 + k:261 + k, lanes]
        return silu(total).astype(BF16)

    for i in (2, 5, 8, 9):
        fetch(i).wait()
    for r in range(2):
        bcall[x, r] = conv(conv_b, bc[r], bc_tail, r, cbw, cbb, slice(0, 128))
    pl.semaphore_wait(bar, len(others) + jnp.where(depth == 3, 4, 0))

    def a2a(b, q):
        return rcopy(
            wsrc.at[b, pl.ds(2 * q, 2)], wfull.at[d_me, pl.ds(2 * q, 2), x],
            a2a_send.at[b, q], a2a_recv.at[x], at(x=2 * c + b, c=q),
        )

    def a2a_local(b, q):
        return jnp.logical_and(x == 2 * c + b, c == q)

    for b in range(2):
        for q in range(2):
            @pl.when(jnp.logical_not(a2a_local(b, q)))
            def _():
                a2a(b, q).start()

            @pl.when(a2a_local(b, q))
            def _():
                wfull[d_me, 2 * q, x] = wsrc[b, 2 * q]
                wfull[d_me, 2 * q + 1, x] = wsrc[b, 2 * q + 1]

    def bc_copy(r, j):
        return rcopy(
            bcall.at[x, r], bcall.at[x, r], bc_send.at[r, j - 1], bc_recv.at[x, r], xn(j)
        )

    for r in range(2):
        for j in (1, 3, 2):
            bc_copy(r, j).start()

    row = lax.broadcasted_iota(jnp.int32, (256, 256), 0)
    col = lax.broadcasted_iota(jnp.int32, (256, 256), 1)
    tril = (row >= col).astype(F32)
    for i in (3, 10, 11):
        fetch(i).wait()
    rate = jnp.exp(a_log[...])

    def prepare(r):
        turned = jnp.concatenate(
            [dt[:, r * 256:(r + 1) * 256], jnp.zeros((120, 256), F32)], axis=0
        )
        v = jnp.transpose(turned)[:, 0:8] + dt_bias[...]
        step = jnp.maximum(v, 0.0) + jnp.log1p(jnp.exp(-jnp.abs(v)))
        ldc[r] = jnp.zeros((256, 128), F32)
        stc[r] = jnp.zeros((256, 128), F32)
        ldc[r, :, 0:8] = jnp.dot(
            tril, -rate * step, precision=HIGHEST, preferred_element_type=F32
        )
        stc[r, :, 0:8] = step
        ldr[r] = jnp.transpose(ldc[r])[0:8]
        stp[r] = jnp.transpose(stc[r])[0:8]
        if r == 0:
            for i in (0, 4, 6, 7):
                fetch(i).wait()
        for p in range(4):
            lanes = slice(p * 128, (p + 1) * 128)
            xact[r, p] = conv(conv_x, xs[r, :, lanes], x_tail, r, cxw, cxb, lanes)

    lane = lax.broadcasted_iota(jnp.int32, (1, 128), 1)
    low = lane < 64
    r128 = lax.broadcasted_iota(jnp.int32, (128, 128), 0)
    c128 = lax.broadcasted_iota(jnp.int32, (128, 128), 1)
    upper = jnp.where(r128 >= c128, 0.0, NEG)

    def pick(table, r, p, rows=slice(None)):
        return jnp.where(
            low, table[r, rows, 2 * p:2 * p + 1], table[r, rows, 2 * p + 1:2 * p + 2]
        )

    def b_rows(r):
        return jnp.concatenate([bcall[0, r], bcall[1, r]], axis=1)

    def ssd(r):
        c_rows = jnp.concatenate([bcall[2, r], bcall[3, r]], axis=1)
        score[...] = dot_nt(c_rows, b_rows(r))
        for p in range(4):
            lanes = slice(p * 128, (p + 1) * 128)
            xp = xact[r, p]
            masked = [jnp.where(low, xp, 0).astype(BF16), jnp.where(low, 0, xp).astype(BF16)]
            top, bottom = [], []
            for e in range(2):
                h = 2 * p + e

                def mix(i, j):
                    ri, rj = slice(i * 128, i * 128 + 128), slice(j * 128, j * 128 + 128)
                    spread = ldc[r, ri, h:h + 1] - ldr[r, h:h + 1, rj]
                    if i == j:
                        spread = spread + upper
                        spread = jnp.minimum(spread, 0.0)
                    return (score[ri, rj] * jnp.exp(spread) * stp[r, h:h + 1, rj]).astype(BF16)

                top.append(mix(0, 0))
                bottom += [mix(1, 0), mix(1, 1)]
            y_top = dot_nn(
                jnp.concatenate(top, axis=1),
                jnp.concatenate([masked[0][:128], masked[1][:128]], axis=0),
            )
            y_bottom = dot_nn(
                jnp.concatenate(bottom, axis=1), jnp.concatenate(masked, axis=0)
            )
            held = state[r, 2 * p:2 * p + 2].reshape(128, 256).astype(BF16)
            from_state = dot_nt(c_rows, held)
            skip = jnp.where(
                low, skip_d[0:1, 2 * p:2 * p + 1], skip_d[0:1, 2 * p + 1:2 * p + 2]
            )
            rows = jnp.concatenate([y_top, y_bottom], axis=0)
            rows = rows + from_state * jnp.exp(pick(ldc, r, p)) + skip * xp.astype(F32)
            gall[r, x, p] = (rows * silu(gate[r, :, lanes].astype(F32))).astype(BF16)

    def state_copy(r):
        return pltpu.make_async_copy(new_state.at[r], state_out.at[r], out_sem.at[r])

    def carry(r):
        for p in range(4):
            last = pick(ldc, r, p, slice(255, 256))
            weight = jnp.exp(last - pick(ldc, r, p)) * pick(stc, r, p)
            xw = (xact[r, p].astype(F32) * weight).astype(BF16)
            update = dot_tn(xw, b_rows(r))
            for e in range(2):
                h = 2 * p + e
                decay = jnp.exp(ldc[r, 255:256, h:h + 1])
                new_state[r, h] = decay * state[r, h] + update[e * 64:(e + 1) * 64]
        state_copy(r).start()

    def y_copy(half, d, s, j):
        piece = wfull.at[d, 2 * c + s]
        return rcopy(piece, piece, y_send.at[half, s, j - 1], w_recv.at[d, s], yn(j))

    def z_copy(s):
        piece = wfull.at[d_me, 2 * c + s]
        return rcopy(piece, piece, z_send.at[s], w_recv.at[d_me, s], opposite)

    def sib_copy(d, s):
        piece = wfull.at[d, 2 * c + s]
        return rcopy(piece, piece, sib_send.at[d, s], sib_recv.at[d, s], sibling)

    def w_wait(d, s):
        piece = wfull.at[d, 2 * c + s]
        rcopy(piece, piece, z_send.at[s], w_recv.at[d, s], opposite).wait_recv()

    def sib_wait(d, s):
        piece = wfull.at[d, 2 * (1 - c) + s]
        rcopy(piece, piece, sib_send.at[d, s], sib_recv.at[d, s], sibling).wait_recv()

    def spread_own():
        for j in range(4):
            @pl.when(jnp.logical_not(jnp.logical_and(x == j, c == x_owner)))
            def _():
                rcopy(
                    wsrc.at[0, pl.ds(0, 2)], wfull.at[d_me, pl.ds(2 * c, 2), j],
                    a2a_send.at[0, 0], a2a_recv.at[j], sibling,
                ).wait_recv()

        for s in range(2):
            z_copy(s).start()
        for s in range(2):
            for j in (1, 3, 2):
                y_copy(0, d_me, s, j).start()
            sib_copy(d_me, s).start()

    def spread_far(s):
        w_wait(d_far, s)
        for j in (1, 3, 2):
            y_copy(1, d_far, s, j).start()
        sib_copy(d_far, s).start()

    def hand_over(half, s):
        for j in (1, 3, 2):
            d = half * 4 + lax.rem(y + j, 4)
            w_wait(d, s)
            sib_copy(d, s).start()

    def sib_all(half):
        for i in range(4):
            for s in range(2):
                sib_wait(half * 4 + i, s)

    def g_copy(r, j):
        return rcopy(gall.at[r, x], gall.at[r, x], g_send.at[r, j - 1], g_recv.at[r, x], xn(j))

    def g_start(r):
        for j in (1, 3, 2):
            g_copy(r, j).start()

    def g_wait(r):
        for j in (1, 3, 2):
            source = lax.rem(x + j, 4)
            slot = gall.at[r, source]
            rcopy(slot, slot, g_send.at[r, j - 1], g_recv.at[r, source], xn(j)).wait_recv()

    def bc_wait(r):
        for j in (1, 3, 2):
            source = lax.rem(x + j, 4)
            slot = bcall.at[source, r]
            rcopy(slot, slot, bc_send.at[r, j - 1], bc_recv.at[source, r], xn(j)).wait_recv()

    def row_factor(r):
        total = jnp.zeros((256, 128), F32)
        for k in range(4):
            for j in range(4):
                block = gall[r, j, k].astype(F32)
                total = total + block * block
        return lax.rsqrt(jnp.sum(total, axis=1, keepdims=True) / 2048.0 + EPS)

    def project(r, half):
        factor = row_factor(r)
        rows = jnp.concatenate([gall[r, j, k] for k in range(4) for j in range(4)], axis=1)
        for i in range(2):
            d = half * 4 + 2 * i
            both = jnp.concatenate(
                [wfull[d].reshape(2048, 128), wfull[d + 1].reshape(2048, 128)], axis=1
            )
            product = dot_nn(rows, both) * factor
            part[r, d] = product[:, :128]
            part[r, d + 1] = product[:, 128:]

    def s_copy(r, d, way, target):
        return rcopy(
            sbuf.at[r, d], rbuf.at[way, r, d], s_send.at[r, d], s_recv.at[way, r, d],
            at(zl=target),
        )

    def s_wait(r, d, way):
        slot = rbuf.at[way, r, d]
        rcopy(slot, slot, s_send.at[r, d], s_recv.at[way, r, d], sibling).wait_recv()

    def relay(r, d, fed, came, way, target):
        @pl.when(fed)
        def _():
            s_wait(r, d, came)
            sbuf[r, d] = (part[r, d] + rbuf[came, r, d].astype(F32)).astype(BF16)

        @pl.when(jnp.logical_not(fed))
        def _():
            sbuf[r, d] = part[r, d].astype(BF16)

        s_copy(r, d, way, target).start()

    def relay_all(r, half):
        @pl.when(half_line == half)
        def _():
            def body(i, carry_):
                flip = lax.div(seat_line, 2)
                near = 3 - (seat_line + flip * (3 - 2 * seat_line))
                spot = jnp.where(i < near, 3 - i, i - near)
                d = half * 4 + spot + flip * (3 - 2 * spot)
                way = (d < zl).astype(jnp.int32)
                fed = seat_line + way * (3 - 2 * seat_line) > 0
                relay(r, d, fed, way, way, zl + 1 - 2 * way)
                return carry_

            lax.fori_loop(0, 3, body, 0)

        @pl.when(half_line != half)
        def _():
            def body(i, carry_):
                d = half * 4 + i + half * (3 - 2 * i)
                last = depth == 3
                target = jnp.where(last, d, zl + 1 - 2 * half_line)
                relay(r, d, depth > 0, 0, jnp.where(last, 2, 0), target)
                return carry_

            lax.fori_loop(0, 4, body, 0)

    def finish(r):
        @pl.when(seat_line > 0)
        def _():
            s_wait(r, zl, 0)
            part[r, zl] = part[r, zl] + rbuf[0, r, zl].astype(F32)

        @pl.when(seat_line < 3)
        def _():
            s_wait(r, zl, 1)
            part[r, zl] = part[r, zl] + rbuf[1, r, zl].astype(F32)

        s_wait(r, zl, 2)
        out[r] = (part[r, zl] + rbuf[2, r, zl].astype(F32)).astype(BF16)

    prepare(0)
    spread_own()
    prepare(1)
    for i in (13, 1, 12):
        fetch(i).wait()
    bc_wait(0)
    ssd(0)
    g_start(0)
    bc_wait(1)
    ssd(1)
    g_start(1)
    for s in range(2):
        hand_over(zh, s)
    carry(0)
    carry(1)
    spread_far(0)
    sib_all(zh)
    g_wait(0)
    project(0, zh)
    relay_all(0, zh)
    g_wait(1)
    project(1, zh)
    relay_all(1, zh)
    hand_over(1 - zh, 0)
    spread_far(1)
    hand_over(1 - zh, 1)
    sib_all(1 - zh)
    project(0, 1 - zh)
    relay_all(0, 1 - zh)
    project(1, 1 - zh)
    relay_all(1, 1 - zh)
    finish(0)
    finish(1)

    for r in range(2):
        state_copy(r).wait()
    for b in range(2):
        for q in range(2):
            @pl.when(jnp.logical_not(a2a_local(b, q)))
            def _():
                a2a(b, q).wait_send()
    for s in range(2):
        z_copy(s).wait_send()
        for j in (1, 2, 3):
            y_copy(0, d_me, s, j).wait_send()
            y_copy(1, d_far, s, j).wait_send()
        for d in range(8):
            sib_copy(d, s).wait_send()
    for r in range(2):
        for j in (1, 2, 3):
            bc_copy(r, j).wait_send()
            g_copy(r, j).wait_send()
        for d in range(8):
            @pl.when(d != zl)
            def _():
                s_copy(r, d, 0, d).wait_send()


def per_device(
    xs_in, gate_in, bc_in, dt_raw, x_tail, bc_tail, conv_x_w, conv_x_b, conv_bc_w, conv_bc_b,
    dt_bias, a_log, skip_d, state_in, norm_gain, out_values, out_scales,
):
    vmem = pl.BlockSpec(memory_space=pltpu.VMEM)
    stay = pl.BlockSpec(memory_space=pltpu.HBM)
    dma = pltpu.SemaphoreType.DMA
    operands = (
        xs_in.reshape(2, 256, 512), gate_in.reshape(2, 256, 512), bc_in.reshape(2, 256, 128),
        dt_raw.T, x_tail.transpose(1, 0, 2), bc_tail.transpose(1, 0, 2), conv_x_w,
        conv_x_b.reshape(1, 512), conv_bc_w, conv_bc_b.reshape(1, 128), dt_bias.reshape(1, 8),
        a_log.reshape(1, 8), skip_d.reshape(1, 8), state_in, norm_gain.reshape(1, 512),
        out_values, out_scales.T,
    )
    out, new_state = pl.pallas_call(
        kernel,
        name="mixer",
        out_shape=(
            jax.ShapeDtypeStruct((2, 256, 128), BF16),
            jax.ShapeDtypeStruct(state_in.shape, F32),
        ),
        in_specs=[stay] * 17,
        out_specs=(vmem, stay),
        scratch_shapes=[pltpu.VMEM(a.shape, a.dtype) for a in operands] + [
            pltpu.VMEM((2, 4, 128, 128), BF16),
            pltpu.VMEM((8, 4, 4, 128, 128), BF16),
            pltpu.VMEM((4, 2, 256, 128), BF16),
            pltpu.VMEM((2, 4, 4, 256, 128), BF16),
            pltpu.VMEM((2, 4, 256, 128), BF16),
            pltpu.VMEM((264, 512), F32),
            pltpu.VMEM((264, 128), F32),
            pltpu.VMEM((2, 256, 128), F32),
            pltpu.VMEM((2, 256, 128), F32),
            pltpu.VMEM((2, 8, 256), F32),
            pltpu.VMEM((2, 8, 256), F32),
            pltpu.VMEM((256, 256), F32),
            pltpu.VMEM((2, 8, 256, 128), F32),
            pltpu.VMEM((2, 8, 256, 128), BF16),
            pltpu.VMEM((3, 2, 8, 256, 128), BF16),
            pltpu.VMEM((2, 8, 64, 256), F32),
            dma((17,)),
            dma((2,)),
            dma((2, 2)),
            dma((4,)),
            dma((2, 2, 3)),
            dma((2,)),
            dma((8, 2)),
            dma((8, 2)),
            dma((8, 2)),
            dma((2, 3)),
            dma((4, 2)),
            dma((2, 3)),
            dma((2, 4)),
            dma((2, 8)),
            dma((3, 2, 8)),
        ],
        compiler_params=pltpu.CompilerParams(
            collective_id=0, has_side_effects=True, vmem_limit_bytes=60 * 1024 * 1024
        ),
    )(*operands)
    return out.reshape(512, 128), new_state


def solution(mesh):
    placed = (
        P("fsdp", "chan"),
        P("fsdp", "chan"),
        P("fsdp", "chan"),
        P("fsdp", "chan"),
        P("fsdp", None, "chan"),
        P("fsdp", None, "chan"),
        P(None, "chan"),
        P("chan"),
        P(None, "chan"),
        P("chan"),
        P("chan"),
        P("chan"),
        P("chan"),
        P("fsdp", "chan", None, None),
        P("chan"),
        P("chan", "fsdp"),
        P("chan", "fsdp"),
    )
    return jax.shard_map(
        per_device,
        mesh=mesh,
        in_specs=placed,
        out_specs=(P("fsdp", "chan"), P("fsdp", "chan", None, None)),
        check_vma=False,
    )
```

```python
import functools

import jax
import jax.numpy as jnp
from jax import lax
from jax.experimental import pallas as pl
from jax.experimental.pallas import tpu as pltpu
from jax.sharding import PartitionSpec as P

EPS = 1e-05
MESH = pl.DeviceIdType.MESH
F32 = jnp.float32
BF16 = jnp.bfloat16
NEG = -1e30
HIGHEST = lax.Precision.HIGHEST


def silu(v):
    return v / (1.0 + jnp.exp(-v))


def dot_nt(a, b):
    return lax.dot_general(a, b, (((1,), (1,)), ((), ())), preferred_element_type=F32)


def dot_tn(a, b):
    return lax.dot_general(a, b, (((0,), (0,)), ((), ())), preferred_element_type=F32)


def dot_nn(a, b):
    return jnp.dot(a, b, preferred_element_type=F32)


def kernel(*refs):
    hbm, (out, state_out), held, refs = refs[:17], refs[17:19], refs[19:36], refs[36:]
    (
        xs, gate, bc, dt, x_tail, bc_tail, cxw, cxb, cbw, cbb, dt_bias, a_log, skip_d, state, gain,
        values, scales,
    ) = held
    (
        wsrc, wfar, wfull, bcall, gall, xact, conv_x, conv_b, ldc, stc, ldr, stp, score, part, sbuf,
        rbuf, new_state, in_sem, out_sem, a2a_send, a2a_recv, y_send, z_send,
        z_recv, w_recv, sib_send, sib_recv, bc_send,
        bc_recv, g_send, g_recv, s_send, s_recv,
    ) = refs
    f = lax.axis_index("fsdp")
    ch = lax.axis_index("chan")
    zh, y, c = lax.div(f, 8), lax.rem(lax.div(f, 2), 4), lax.rem(f, 2)
    zl, x = lax.div(ch, 4), lax.rem(ch, 4)
    x_owner = lax.div(x, 2)
    d_me = zh * 4 + y
    d_far = (1 - zh) * 4 + y

    def at(zh=zh, y=y, c=c, zl=zl, x=x):
        return ((zh * 4 + y) * 2 + c, zl * 4 + x)

    def xn(j, core=c):
        return at(x=lax.rem(x + j, 4), c=core)

    def yn(j):
        return at(y=lax.rem(y + j, 4))

    def zn(step):
        z = lax.rem(zh * 8 + zl + step, 16)
        return at(zh=lax.div(z, 8), zl=lax.rem(z, 8))

    sibling = at(c=1 - c)
    opposite = at(zh=1 - zh)

    def rcopy(src, dst, send, recv, device):
        return pltpu.make_async_remote_copy(
            src_ref=src, dst_ref=dst, send_sem=send, recv_sem=recv, device_id=device,
            device_id_type=MESH,
        )

    bar = pltpu.get_barrier_semaphore()
    half_line, seat_line = lax.div(zl, 4), lax.rem(zl, 4)
    depth = seat_line + half_line * (3 - 2 * seat_line)
    others = [xn(j, core) for j in (1, 2, 3) for core in (c, 1 - c)]
    others += [yn(j) for j in (1, 2, 3)] + [zn(1), zn(15), opposite, sibling]
    for device in others + [at(zl=4 - half_line)]:
        pl.semaphore_signal(bar, inc=1, device_id=device, device_id_type=MESH)

    def fetch(i):
        return pltpu.make_async_copy(hbm[i], held[i], in_sem.at[i])

    for i in (15, 14, 16, 2, 5, 8, 9, 3, 10, 11, 0, 4, 6, 7, 13, 1, 12):
        fetch(i).start()

    for i in (15, 14, 16):
        fetch(i).wait()
    gain_rows = jnp.transpose(jnp.broadcast_to(gain[...], (128, 512)))
    for k in range(4):
        for b in range(2):
            tile = values[k * 128:(k + 1) * 128, b * 128:(b + 1) * 128].astype(F32)
            tile = tile * scales[b:b + 1, k:k + 1] * gain_rows[k * 128:(k + 1) * 128]
            wsrc[k % 2, b, k // 2] = tile.astype(BF16)

    def conv(scratch, rows, tails, r, w, b, lanes):
        for k in range(3):
            scratch[5 + k:6 + k, lanes] = tails[k].astype(F32)[r:r + 1, lanes]
        scratch[8:264, lanes] = rows.astype(F32)
        total = b[:, lanes]
        for k in range(4):
            total = total + w[k:k + 1, lanes] * scratch[5 + k:261 + k, lanes]
        return silu(total).astype(BF16)

    for i in (2, 5, 8, 9):
        fetch(i).wait()
    for r in range(2):
        bcall[x, r] = conv(conv_b, bc[r], bc_tail, r, cbw, cbb, slice(0, 128))
    pl.semaphore_wait(bar, len(others) + jnp.where(depth == 3, 4, 0))

    def z_copy(s):
        return rcopy(wsrc.at[s], wfar.at[s], z_send.at[s], z_recv.at[s], opposite)

    def a2a(half, s, b, q):
        source, d = ((wsrc, d_me), (wfar, d_far))[half]
        return rcopy(
            source.at[s, b, q], wfull.at[d, 2 * q + s, x], a2a_send.at[half, s, b, q],
            a2a_recv.at[half, s, x], at(x=2 * c + b, c=q),
        )

    def a2a_local(b, q):
        return jnp.logical_and(x == 2 * c + b, c == q)

    def a2a_start(half, s):
        source, d = ((wsrc, d_me), (wfar, d_far))[half]
        for b in range(2):
            for q in range(2):
                @pl.when(jnp.logical_not(a2a_local(b, q)))
                def _():
                    a2a(half, s, b, q).start()

                @pl.when(a2a_local(b, q))
                def _():
                    wfull[d, 2 * q + s, x] = source[s, b, q]

    def a2a_wait(half, s):
        d = (d_me, d_far)[half]
        for j in range(4):
            @pl.when(jnp.logical_not(jnp.logical_and(x == j, c == x_owner)))
            def _():
                slot = wfull.at[d, 2 * c + s, j]
                rcopy(
                    slot, slot, a2a_send.at[half, s, 0, 0], a2a_recv.at[half, s, j], sibling
                ).wait_recv()

    def bc_copy(r, j):
        return rcopy(
            bcall.at[x, r], bcall.at[x, r], bc_send.at[r, j - 1], bc_recv.at[x, r], xn(j)
        )

    def bc_start(r):
        for j in (1, 3, 2):
            bc_copy(r, j).start()

    bc_start(0)
    z_copy(0).start()
    for s in range(2):
        a2a_start(0, s)

    row = lax.broadcasted_iota(jnp.int32, (256, 256), 0)
    col = lax.broadcasted_iota(jnp.int32, (256, 256), 1)
    tril = (row >= col).astype(F32)
    for i in (3, 10, 11):
        fetch(i).wait()
    rate = jnp.exp(a_log[...])

    def prepare(r):
        turned = jnp.concatenate(
            [dt[:, r * 256:(r + 1) * 256], jnp.zeros((120, 256), F32)], axis=0
        )
        v = jnp.transpose(turned)[:, 0:8] + dt_bias[...]
        step = jnp.maximum(v, 0.0) + jnp.log1p(jnp.exp(-jnp.abs(v)))
        ldc[r] = jnp.zeros((256, 128), F32)
        stc[r] = jnp.zeros((256, 128), F32)
        ldc[r, :, 0:8] = jnp.dot(
            tril, -rate * step, precision=HIGHEST, preferred_element_type=F32
        )
        stc[r, :, 0:8] = step
        ldr[r] = jnp.transpose(ldc[r])[0:8]
        stp[r] = jnp.transpose(stc[r])[0:8]
        if r == 0:
            for i in (0, 4, 6, 7):
                fetch(i).wait()
        for p in range(4):
            lanes = slice(p * 128, (p + 1) * 128)
            xact[r, p] = conv(conv_x, xs[r, :, lanes], x_tail, r, cxw, cxb, lanes)

    lane = lax.broadcasted_iota(jnp.int32, (1, 128), 1)
    low = lane < 64
    r128 = lax.broadcasted_iota(jnp.int32, (128, 128), 0)
    c128 = lax.broadcasted_iota(jnp.int32, (128, 128), 1)
    upper = jnp.where(r128 >= c128, 0.0, NEG)

    def pick(table, r, p, rows=slice(None)):
        return jnp.where(
            low, table[r, rows, 2 * p:2 * p + 1], table[r, rows, 2 * p + 1:2 * p + 2]
        )

    def b_rows(r):
        return jnp.concatenate([bcall[0, r], bcall[1, r]], axis=1)

    def ssd(r):
        c_rows = jnp.concatenate([bcall[2, r], bcall[3, r]], axis=1)
        score[...] = dot_nt(c_rows, b_rows(r))
        for p in range(4):
            lanes = slice(p * 128, (p + 1) * 128)
            xp = xact[r, p]
            masked = [jnp.where(low, xp, 0).astype(BF16), jnp.where(low, 0, xp).astype(BF16)]
            top, bottom = [], []
            for e in range(2):
                h = 2 * p + e

                def mix(i, j):
                    ri, rj = slice(i * 128, i * 128 + 128), slice(j * 128, j * 128 + 128)
                    spread = ldc[r, ri, h:h + 1] - ldr[r, h:h + 1, rj]
                    if i == j:
                        spread = spread + upper
                        spread = jnp.minimum(spread, 0.0)
                    return (score[ri, rj] * jnp.exp(spread) * stp[r, h:h + 1, rj]).astype(BF16)

                top.append(mix(0, 0))
                bottom += [mix(1, 0), mix(1, 1)]
            y_top = dot_nn(
                jnp.concatenate(top, axis=1),
                jnp.concatenate([masked[0][:128], masked[1][:128]], axis=0),
            )
            y_bottom = dot_nn(
                jnp.concatenate(bottom, axis=1), jnp.concatenate(masked, axis=0)
            )
            held = state[r, 2 * p:2 * p + 2].reshape(128, 256).astype(BF16)
            from_state = dot_nt(c_rows, held)
            skip = jnp.where(
                low, skip_d[0:1, 2 * p:2 * p + 1], skip_d[0:1, 2 * p + 1:2 * p + 2]
            )
            rows = jnp.concatenate([y_top, y_bottom], axis=0)
            rows = rows + from_state * jnp.exp(pick(ldc, r, p)) + skip * xp.astype(F32)
            gall[r, x, p] = (rows * silu(gate[r, :, lanes].astype(F32))).astype(BF16)

    def state_copy(r):
        return pltpu.make_async_copy(new_state.at[r], state_out.at[r], out_sem.at[r])

    def carry(r):
        for p in range(4):
            last = pick(ldc, r, p, slice(255, 256))
            weight = jnp.exp(last - pick(ldc, r, p)) * pick(stc, r, p)
            xw = (xact[r, p].astype(F32) * weight).astype(BF16)
            update = dot_tn(xw, b_rows(r))
            for e in range(2):
                h = 2 * p + e
                decay = jnp.exp(ldc[r, 255:256, h:h + 1])
                new_state[r, h] = decay * state[r, h] + update[e * 64:(e + 1) * 64]
        state_copy(r).start()

    def y_copy(half, d, s, j):
        piece = wfull.at[d, 2 * c + s]
        return rcopy(piece, piece, y_send.at[half, s, j - 1], w_recv.at[d, s], yn(j))

    def sib_copy(d, s):
        piece = wfull.at[d, 2 * c + s]
        return rcopy(piece, piece, sib_send.at[d, s], sib_recv.at[d, s], sibling)

    def w_wait(d, s):
        piece = wfull.at[d, 2 * c + s]
        rcopy(piece, piece, sib_send.at[d, s], w_recv.at[d, s], sibling).wait_recv()

    def sib_wait(d, s):
        piece = wfull.at[d, 2 * (1 - c) + s]
        rcopy(piece, piece, sib_send.at[d, s], sib_recv.at[d, s], sibling).wait_recv()

    def spread(half, s):
        a2a_wait(half, s)
        d = (d_me, d_far)[half]
        for j in (1, 3, 2):
            y_copy(half, d, s, j).start()
        sib_copy(d, s).start()

    def far_start(s):
        z_copy(s).wait_recv()
        a2a_start(1, s)

    def hand_over(half, s):
        for j in (1, 3, 2):
            d = half * 4 + lax.rem(y + j, 4)
            w_wait(d, s)
            sib_copy(d, s).start()

    def sib_all(half):
        for i in range(4):
            for s in range(2):
                sib_wait(half * 4 + i, s)

    def g_copy(r, j):
        return rcopy(gall.at[r, x], gall.at[r, x], g_send.at[r, j - 1], g_recv.at[r, x], xn(j))

    def g_start(r):
        for j in (1, 3, 2):
            g_copy(r, j).start()

    def g_wait(r):
        for j in (1, 3, 2):
            source = lax.rem(x + j, 4)
            slot = gall.at[r, source]
            rcopy(slot, slot, g_send.at[r, j - 1], g_recv.at[r, source], xn(j)).wait_recv()

    def bc_wait(r):
        for j in (1, 3, 2):
            source = lax.rem(x + j, 4)
            slot = bcall.at[source, r]
            rcopy(slot, slot, bc_send.at[r, j - 1], bc_recv.at[source, r], xn(j)).wait_recv()

    def row_factor(r):
        total = jnp.zeros((256, 128), F32)
        for k in range(4):
            for j in range(4):
                block = gall[r, j, k].astype(F32)
                total = total + block * block
        return lax.rsqrt(jnp.sum(total, axis=1, keepdims=True) / 2048.0 + EPS)

    def project(r, half):
        factor = row_factor(r)
        rows = jnp.concatenate([gall[r, j, k] for k in range(4) for j in range(4)], axis=1)
        for i in range(2):
            d = half * 4 + 2 * i
            both = jnp.concatenate(
                [wfull[d].reshape(2048, 128), wfull[d + 1].reshape(2048, 128)], axis=1
            )
            product = dot_nn(rows, both) * factor
            for u in range(2):
                part[2 * r + u, d] = product[u * 128:(u + 1) * 128, :128]
                part[2 * r + u, d + 1] = product[u * 128:(u + 1) * 128, 128:]

    def s_copy(r, d, way, target):
        return rcopy(
            sbuf.at[r, d], rbuf.at[way, r, d], s_send.at[r, d], s_recv.at[way, r, d],
            at(zl=target),
        )

    def s_wait(r, d, way):
        slot = rbuf.at[way, r, d]
        rcopy(slot, slot, s_send.at[r, d], s_recv.at[way, r, d], sibling).wait_recv()

    def relay(r, d, fed, came, way, target):
        @pl.when(fed)
        def _():
            s_wait(r, d, came)
            sbuf[r, d] = (part[r, d] + rbuf[came, r, d].astype(F32)).astype(BF16)

        @pl.when(jnp.logical_not(fed))
        def _():
            sbuf[r, d] = part[r, d].astype(BF16)

        s_copy(r, d, way, target).start()

    def relay_all(r, half):
        @pl.when(half_line == half)
        def _():
            def body(i, carry_):
                flip = lax.div(seat_line, 2)
                near = 3 - (seat_line + flip * (3 - 2 * seat_line))
                spot = jnp.where(i < near, 3 - i, i - near)
                d = half * 4 + spot + flip * (3 - 2 * spot)
                way = (d < zl).astype(jnp.int32)
                fed = seat_line + way * (3 - 2 * seat_line) > 0
                for u in range(2):
                    relay(2 * r + u, d, fed, way, way, zl + 1 - 2 * way)
                return carry_

            lax.fori_loop(0, 3, body, 0)

        @pl.when(half_line != half)
        def _():
            def body(i, carry_):
                d = half * 4 + i + half * (3 - 2 * i)
                last = depth == 3
                target = jnp.where(last, d, zl + 1 - 2 * half_line)
                for u in range(2):
                    relay(2 * r + u, d, depth > 0, 0, jnp.where(last, 2, 0), target)
                return carry_

            lax.fori_loop(0, 4, body, 0)

    def finish(r):
        @pl.when(seat_line > 0)
        def _():
            s_wait(r, zl, 0)
            part[r, zl] = part[r, zl] + rbuf[0, r, zl].astype(F32)

        @pl.when(seat_line < 3)
        def _():
            s_wait(r, zl, 1)
            part[r, zl] = part[r, zl] + rbuf[1, r, zl].astype(F32)

        s_wait(r, zl, 2)
        out[r // 2, r % 2 * 128:r % 2 * 128 + 128] = (
            part[r, zl] + rbuf[2, r, zl].astype(F32)
        ).astype(BF16)

    prepare(0)
    bc_start(1)
    prepare(1)
    for i in (13, 1, 12):
        fetch(i).wait()
    bc_wait(0)
    ssd(0)
    g_start(0)
    spread(0, 0)
    spread(0, 1)
    bc_wait(1)
    ssd(1)
    z_copy(0).wait_send()
    z_copy(1).start()
    far_start(0)
    hand_over(zh, 0)
    hand_over(zh, 1)
    carry(0)
    for j in (1, 2, 3):
        g_copy(0, j).wait_send()
    g_start(1)
    spread(1, 0)
    carry(1)
    sib_all(zh)
    far_start(1)
    g_wait(0)
    project(0, zh)
    relay_all(0, zh)
    spread(1, 1)
    hand_over(1 - zh, 0)
    g_wait(1)
    project(1, zh)
    relay_all(1, zh)
    hand_over(1 - zh, 1)
    sib_all(1 - zh)
    project(0, 1 - zh)
    relay_all(0, 1 - zh)
    project(1, 1 - zh)
    relay_all(1, 1 - zh)
    for r in range(4):
        finish(r)

    for r in range(2):
        state_copy(r).wait()
    for b in range(2):
        for q in range(2):
            @pl.when(jnp.logical_not(a2a_local(b, q)))
            def _():
                for half in range(2):
                    for s in range(2):
                        a2a(half, s, b, q).wait_send()
    for s in range(2):
        if s == 1:
            z_copy(s).wait_send()
        for j in (1, 2, 3):
            y_copy(0, d_me, s, j).wait_send()
            y_copy(1, d_far, s, j).wait_send()
        for d in range(8):
            sib_copy(d, s).wait_send()
    for r in range(2):
        for j in (1, 2, 3):
            bc_copy(r, j).wait_send()
            if r == 1:
                g_copy(r, j).wait_send()
    for r in range(4):
        for d in range(8):
            @pl.when(d != zl)
            def _():
                s_copy(r, d, 0, d).wait_send()


def per_device(
    xs_in, gate_in, bc_in, dt_raw, x_tail, bc_tail, conv_x_w, conv_x_b, conv_bc_w, conv_bc_b,
    dt_bias, a_log, skip_d, state_in, norm_gain, out_values, out_scales,
):
    vmem = pl.BlockSpec(memory_space=pltpu.VMEM)
    stay = pl.BlockSpec(memory_space=pltpu.HBM)
    dma = pltpu.SemaphoreType.DMA
    operands = (
        xs_in.reshape(2, 256, 512), gate_in.reshape(2, 256, 512), bc_in.reshape(2, 256, 128),
        dt_raw.T, x_tail.transpose(1, 0, 2), bc_tail.transpose(1, 0, 2), conv_x_w,
        conv_x_b.reshape(1, 512), conv_bc_w, conv_bc_b.reshape(1, 128), dt_bias.reshape(1, 8),
        a_log.reshape(1, 8), skip_d.reshape(1, 8), state_in, norm_gain.reshape(1, 512),
        out_values, out_scales.T,
    )
    out, new_state = pl.pallas_call(
        kernel,
        name="mixer",
        out_shape=(
            jax.ShapeDtypeStruct((2, 256, 128), BF16),
            jax.ShapeDtypeStruct(state_in.shape, F32),
        ),
        in_specs=[stay] * 17,
        out_specs=(vmem, stay),
        scratch_shapes=[pltpu.VMEM(a.shape, a.dtype) for a in operands] + [
            pltpu.VMEM((2, 2, 2, 128, 128), BF16),
            pltpu.VMEM((2, 2, 2, 128, 128), BF16),
            pltpu.VMEM((8, 4, 4, 128, 128), BF16),
            pltpu.VMEM((4, 2, 256, 128), BF16),
            pltpu.VMEM((2, 4, 4, 256, 128), BF16),
            pltpu.VMEM((2, 4, 256, 128), BF16),
            pltpu.VMEM((264, 512), F32),
            pltpu.VMEM((264, 128), F32),
            pltpu.VMEM((2, 256, 128), F32),
            pltpu.VMEM((2, 256, 128), F32),
            pltpu.VMEM((2, 8, 256), F32),
            pltpu.VMEM((2, 8, 256), F32),
            pltpu.VMEM((256, 256), F32),
            pltpu.VMEM((4, 8, 128, 128), F32),
            pltpu.VMEM((4, 8, 128, 128), BF16),
            pltpu.VMEM((3, 4, 8, 128, 128), BF16),
            pltpu.VMEM((2, 8, 64, 256), F32),
            dma((17,)),
            dma((2,)),
            dma((2, 2, 2, 2)),
            dma((2, 2, 4)),
            dma((2, 2, 3)),
            dma((2,)),
            dma((2,)),
            dma((8, 2)),
            dma((8, 2)),
            dma((8, 2)),
            dma((2, 3)),
            dma((4, 2)),
            dma((2, 3)),
            dma((2, 4)),
            dma((4, 8)),
            dma((3, 4, 8)),
        ],
        compiler_params=pltpu.CompilerParams(
            collective_id=0, has_side_effects=True, vmem_limit_bytes=60 * 1024 * 1024
        ),
    )(*operands)
    return out.reshape(512, 128), new_state


def solution(mesh):
    placed = (
        P("fsdp", "chan"),
        P("fsdp", "chan"),
        P("fsdp", "chan"),
        P("fsdp", "chan"),
        P("fsdp", None, "chan"),
        P("fsdp", None, "chan"),
        P(None, "chan"),
        P("chan"),
        P(None, "chan"),
        P("chan"),
        P("chan"),
        P("chan"),
        P("chan"),
        P("fsdp", "chan", None, None),
        P("chan"),
        P("chan", "fsdp"),
        P("chan", "fsdp"),
    )
    return jax.shard_map(
        per_device,
        mesh=mesh,
        in_specs=placed,
        out_specs=(P("fsdp", "chan"), P("fsdp", "chan", None, None)),
        check_vma=False,
    )
```

```python
import functools

import jax
import jax.numpy as jnp
from jax import lax
from jax.experimental import pallas as pl
from jax.experimental.pallas import tpu as pltpu
from jax.sharding import PartitionSpec as P

EPS = 1e-05
MESH = pl.DeviceIdType.MESH
F32 = jnp.float32
BF16 = jnp.bfloat16
NEG = -1e30
HIGHEST = lax.Precision.HIGHEST


def silu(v):
    return v / (1.0 + jnp.exp(-v))


def dot_nt(a, b):
    return lax.dot_general(a, b, (((1,), (1,)), ((), ())), preferred_element_type=F32)


def dot_tn(a, b):
    return lax.dot_general(a, b, (((0,), (0,)), ((), ())), preferred_element_type=F32)


def dot_nn(a, b):
    return jnp.dot(a, b, preferred_element_type=F32)


def kernel(*refs):
    hbm, (out, state_out), held, refs = refs[:17], refs[17:19], refs[19:36], refs[36:]
    (
        xs, gate, bc, dt, x_tail, bc_tail, cxw, cxb, cbw, cbb, dt_bias, a_log, skip_d, state, gain,
        values, scales,
    ) = held
    (
        wsrc, wfar, wfull, bcall, gall, xact, conv_x, conv_b, ldc, stc, ldr, stp, score, part, sbuf,
        rbuf, new_state, in_sem, out_sem, a2a_send, a2a_recv, y_send, z_send,
        z_recv, w_recv, sib_send, sib_recv, bc_send,
        bc_recv, g_send, g_recv, s_send, s_recv,
    ) = refs
    f = lax.axis_index("fsdp")
    ch = lax.axis_index("chan")
    zh, y, c = lax.div(f, 8), lax.rem(lax.div(f, 2), 4), lax.rem(f, 2)
    zl, x = lax.div(ch, 4), lax.rem(ch, 4)
    x_owner = lax.div(x, 2)
    d_me = zh * 4 + y
    d_far = (1 - zh) * 4 + y

    def at(zh=zh, y=y, c=c, zl=zl, x=x):
        return ((zh * 4 + y) * 2 + c, zl * 4 + x)

    def xn(j, core=c):
        return at(x=lax.rem(x + j, 4), c=core)

    def yn(j):
        return at(y=lax.rem(y + j, 4))

    def zn(step):
        z = lax.rem(zh * 8 + zl + step, 16)
        return at(zh=lax.div(z, 8), zl=lax.rem(z, 8))

    sibling = at(c=1 - c)
    opposite = at(zh=1 - zh)

    def rcopy(src, dst, send, recv, device):
        return pltpu.make_async_remote_copy(
            src_ref=src, dst_ref=dst, send_sem=send, recv_sem=recv, device_id=device,
            device_id_type=MESH,
        )

    bar = pltpu.get_barrier_semaphore()
    half_line, seat_line = lax.div(zl, 4), lax.rem(zl, 4)
    depth = seat_line + half_line * (3 - 2 * seat_line)
    others = [xn(j, core) for j in (1, 2, 3) for core in (c, 1 - c)]
    others += [yn(j) for j in (1, 2, 3)] + [zn(1), zn(15), opposite, sibling]
    for device in others + [at(zl=4 - half_line)]:
        pl.semaphore_signal(bar, inc=1, device_id=device, device_id_type=MESH)

    def fetch(i):
        return pltpu.make_async_copy(hbm[i], held[i], in_sem.at[i])

    for i in (15, 14, 16, 2, 5, 8, 9, 3, 10, 11, 0, 4, 6, 7, 13, 1, 12):
        fetch(i).start()

    for i in (15, 14, 16):
        fetch(i).wait()
    gain_rows = jnp.transpose(jnp.broadcast_to(gain[...], (128, 512)))
    for k in range(4):
        for b in range(2):
            tile = values[k * 128:(k + 1) * 128, b * 128:(b + 1) * 128].astype(F32)
            tile = tile * scales[b:b + 1, k:k + 1] * gain_rows[k * 128:(k + 1) * 128]
            wsrc[k % 2, b, k // 2] = tile.astype(BF16)

    def conv(scratch, rows, tails, r, w, b, lanes):
        for k in range(3):
            scratch[5 + k:6 + k, lanes] = tails[k].astype(F32)[r:r + 1, lanes]
        scratch[8:264, lanes] = rows.astype(F32)
        total = b[:, lanes]
        for k in range(4):
            total = total + w[k:k + 1, lanes] * scratch[5 + k:261 + k, lanes]
        return silu(total).astype(BF16)

    for i in (2, 5, 8, 9):
        fetch(i).wait()
    for r in range(2):
        bcall[x, r] = conv(conv_b, bc[r], bc_tail, r, cbw, cbb, slice(0, 128))
    pl.semaphore_wait(bar, len(others) + jnp.where(depth == 3, 4, 0))

    def z_copy(s):
        return rcopy(wsrc.at[s], wfar.at[s], z_send.at[s], z_recv.at[s], opposite)

    def a2a(half, s, b, q):
        source, d = ((wsrc, d_me), (wfar, d_far))[half]
        return rcopy(
            source.at[s, b, q], wfull.at[d, 2 * q + s, x], a2a_send.at[half, s, b, q],
            a2a_recv.at[half, s, x], at(x=2 * c + b, c=q),
        )

    def a2a_local(b, q):
        return jnp.logical_and(x == 2 * c + b, c == q)

    def a2a_start(half, s):
        source, d = ((wsrc, d_me), (wfar, d_far))[half]
        for b in range(2):
            for q in range(2):
                @pl.when(jnp.logical_not(a2a_local(b, q)))
                def _():
                    a2a(half, s, b, q).start()

                @pl.when(a2a_local(b, q))
                def _():
                    wfull[d, 2 * q + s, x] = source[s, b, q]

    def a2a_wait(half, s):
        d = (d_me, d_far)[half]
        for j in range(4):
            @pl.when(jnp.logical_not(jnp.logical_and(x == j, c == x_owner)))
            def _():
                slot = wfull.at[d, 2 * c + s, j]
                rcopy(
                    slot, slot, a2a_send.at[half, s, 0, 0], a2a_recv.at[half, s, j], sibling
                ).wait_recv()

    def bc_copy(r, j):
        return rcopy(
            bcall.at[x, r], bcall.at[x, r], bc_send.at[r, j - 1], bc_recv.at[x, r], xn(j)
        )

    def bc_start(r):
        for j in (1, 3, 2):
            bc_copy(r, j).start()

    bc_start(0)
    z_copy(0).start()
    for s in range(2):
        a2a_start(0, s)

    row = lax.broadcasted_iota(jnp.int32, (256, 256), 0)
    col = lax.broadcasted_iota(jnp.int32, (256, 256), 1)
    tril = (row >= col).astype(F32)
    for i in (3, 10, 11):
        fetch(i).wait()
    rate = jnp.exp(a_log[...])

    def prepare(r):
        turned = jnp.concatenate(
            [dt[:, r * 256:(r + 1) * 256], jnp.zeros((120, 256), F32)], axis=0
        )
        v = jnp.transpose(turned)[:, 0:8] + dt_bias[...]
        step = jnp.maximum(v, 0.0) + jnp.log1p(jnp.exp(-jnp.abs(v)))
        ldc[r] = jnp.zeros((256, 128), F32)
        stc[r] = jnp.zeros((256, 128), F32)
        ldc[r, :, 0:8] = jnp.dot(
            tril, -rate * step, precision=HIGHEST, preferred_element_type=F32
        )
        stc[r, :, 0:8] = step
        ldr[r] = jnp.transpose(ldc[r])[0:8]
        stp[r] = jnp.transpose(stc[r])[0:8]
        if r == 0:
            for i in (0, 4, 6, 7):
                fetch(i).wait()
        for p in range(4):
            lanes = slice(p * 128, (p + 1) * 128)
            xact[r, p] = conv(conv_x, xs[r, :, lanes], x_tail, r, cxw, cxb, lanes)

    lane = lax.broadcasted_iota(jnp.int32, (1, 128), 1)
    low = lane < 64
    r128 = lax.broadcasted_iota(jnp.int32, (128, 128), 0)
    c128 = lax.broadcasted_iota(jnp.int32, (128, 128), 1)
    upper = jnp.where(r128 >= c128, 0.0, NEG)

    def pick(table, r, p, rows=slice(None)):
        return jnp.where(
            low, table[r, rows, 2 * p:2 * p + 1], table[r, rows, 2 * p + 1:2 * p + 2]
        )

    def b_rows(r):
        return jnp.concatenate([bcall[0, r], bcall[1, r]], axis=1)

    def ssd(r):
        c_rows = jnp.concatenate([bcall[2, r], bcall[3, r]], axis=1)
        score[...] = dot_nt(c_rows, b_rows(r))
        for p in range(4):
            lanes = slice(p * 128, (p + 1) * 128)
            xp = xact[r, p]
            masked = [jnp.where(low, xp, 0).astype(BF16), jnp.where(low, 0, xp).astype(BF16)]
            top, bottom = [], []
            for e in range(2):
                h = 2 * p + e

                def mix(i, j):
                    ri, rj = slice(i * 128, i * 128 + 128), slice(j * 128, j * 128 + 128)
                    spread = ldc[r, ri, h:h + 1] - ldr[r, h:h + 1, rj]
                    if i == j:
                        spread = spread + upper
                        spread = jnp.minimum(spread, 0.0)
                    return (score[ri, rj] * jnp.exp(spread) * stp[r, h:h + 1, rj]).astype(BF16)

                top.append(mix(0, 0))
                bottom += [mix(1, 0), mix(1, 1)]
            y_top = dot_nn(
                jnp.concatenate(top, axis=1),
                jnp.concatenate([masked[0][:128], masked[1][:128]], axis=0),
            )
            y_bottom = dot_nn(
                jnp.concatenate(bottom, axis=1), jnp.concatenate(masked, axis=0)
            )
            held = state[r, 2 * p:2 * p + 2].reshape(128, 256).astype(BF16)
            from_state = dot_nt(c_rows, held)
            skip = jnp.where(
                low, skip_d[0:1, 2 * p:2 * p + 1], skip_d[0:1, 2 * p + 1:2 * p + 2]
            )
            rows = jnp.concatenate([y_top, y_bottom], axis=0)
            rows = rows + from_state * jnp.exp(pick(ldc, r, p)) + skip * xp.astype(F32)
            gall[r, x, p] = (rows * silu(gate[r, :, lanes].astype(F32))).astype(BF16)

    def state_copy(r):
        return pltpu.make_async_copy(new_state.at[r], state_out.at[r], out_sem.at[r])

    def carry(r):
        for p in range(4):
            last = pick(ldc, r, p, slice(255, 256))
            weight = jnp.exp(last - pick(ldc, r, p)) * pick(stc, r, p)
            xw = (xact[r, p].astype(F32) * weight).astype(BF16)
            update = dot_tn(xw, b_rows(r))
            for e in range(2):
                h = 2 * p + e
                decay = jnp.exp(ldc[r, 255:256, h:h + 1])
                new_state[r, h] = decay * state[r, h] + update[e * 64:(e + 1) * 64]
        state_copy(r).start()

    def y_copy(half, d, s, j):
        piece = wfull.at[d, 2 * c + s]
        return rcopy(piece, piece, y_send.at[half, s, j - 1], w_recv.at[d, s], yn(j))

    def sib_copy(d, s):
        piece = wfull.at[d, 2 * c + s]
        return rcopy(piece, piece, sib_send.at[d, s], sib_recv.at[d, s], sibling)

    def w_wait(d, s):
        piece = wfull.at[d, 2 * c + s]
        rcopy(piece, piece, sib_send.at[d, s], w_recv.at[d, s], sibling).wait_recv()

    def sib_wait(d, s):
        piece = wfull.at[d, 2 * (1 - c) + s]
        rcopy(piece, piece, sib_send.at[d, s], sib_recv.at[d, s], sibling).wait_recv()

    def spread(half, s):
        a2a_wait(half, s)
        d = (d_me, d_far)[half]
        for j in (2, 1, 3):
            y_copy(half, d, s, j).start()
        sib_copy(d, s).start()

    def far_start(s):
        z_copy(s).wait_recv()
        a2a_start(1, s)

    def hand_over(half, s):
        for j in (1, 3, 2):
            d = half * 4 + lax.rem(y + j, 4)
            w_wait(d, s)
            sib_copy(d, s).start()

    def sib_all(half):
        for i in range(4):
            for s in range(2):
                sib_wait(half * 4 + i, s)

    def g_copy(r, j):
        return rcopy(gall.at[r, x], gall.at[r, x], g_send.at[r, j - 1], g_recv.at[r, x], xn(j))

    def g_start(r):
        for j in (2, 1, 3):
            g_copy(r, j).start()

    def g_wait(r):
        for j in (1, 3, 2):
            source = lax.rem(x + j, 4)
            slot = gall.at[r, source]
            rcopy(slot, slot, g_send.at[r, j - 1], g_recv.at[r, source], xn(j)).wait_recv()

    def bc_wait(r):
        for j in (1, 3, 2):
            source = lax.rem(x + j, 4)
            slot = bcall.at[source, r]
            rcopy(slot, slot, bc_send.at[r, j - 1], bc_recv.at[source, r], xn(j)).wait_recv()

    def row_factor(r):
        total = jnp.zeros((256, 128), F32)
        for k in range(4):
            for j in range(4):
                block = gall[r, j, k].astype(F32)
                total = total + block * block
        return lax.rsqrt(jnp.sum(total, axis=1, keepdims=True) / 2048.0 + EPS)

    def project(r, half):
        factor = row_factor(r)
        rows = jnp.concatenate([gall[r, j, k] for k in range(4) for j in range(4)], axis=1)
        for i in range(2):
            d = half * 4 + 2 * i
            both = jnp.concatenate(
                [wfull[d].reshape(2048, 128), wfull[d + 1].reshape(2048, 128)], axis=1
            )
            product = dot_nn(rows, both) * factor
            for u in range(2):
                part[2 * r + u, d] = product[u * 128:(u + 1) * 128, :128]
                part[2 * r + u, d + 1] = product[u * 128:(u + 1) * 128, 128:]

    def s_copy(r, d, way, target):
        return rcopy(
            sbuf.at[r, d], rbuf.at[way, r, d], s_send.at[r, d], s_recv.at[way, r, d],
            at(zl=target),
        )

    def s_wait(r, d, way):
        slot = rbuf.at[way, r, d]
        rcopy(slot, slot, s_send.at[r, d], s_recv.at[way, r, d], sibling).wait_recv()

    def relay(r, d, fed, came, way, target):
        @pl.when(fed)
        def _():
            s_wait(r, d, came)
            sbuf[r, d] = (part[r, d] + rbuf[came, r, d].astype(F32)).astype(BF16)

        @pl.when(jnp.logical_not(fed))
        def _():
            sbuf[r, d] = part[r, d].astype(BF16)

        s_copy(r, d, way, target).start()

    def relay_all(r, half):
        @pl.when(half_line == half)
        def _():
            def body(i, carry_):
                flip = lax.div(seat_line, 2)
                near = 3 - (seat_line + flip * (3 - 2 * seat_line))
                spot = jnp.where(i < near, 3 - i, i - near)
                d = half * 4 + spot + flip * (3 - 2 * spot)
                way = (d < zl).astype(jnp.int32)
                fed = seat_line + way * (3 - 2 * seat_line) > 0
                for u in range(2):
                    relay(2 * r + u, d, fed, way, way, zl + 1 - 2 * way)
                return carry_

            lax.fori_loop(0, 3, body, 0)

        @pl.when(half_line != half)
        def _():
            def body(i, carry_):
                d = half * 4 + i + half * (3 - 2 * i)
                last = depth == 3
                target = jnp.where(last, d, zl + 1 - 2 * half_line)
                for u in range(2):
                    relay(2 * r + u, d, depth > 0, 0, jnp.where(last, 2, 0), target)
                return carry_

            lax.fori_loop(0, 4, body, 0)

    def finish(r):
        @pl.when(seat_line > 0)
        def _():
            s_wait(r, zl, 0)
            part[r, zl] = part[r, zl] + rbuf[0, r, zl].astype(F32)

        @pl.when(seat_line < 3)
        def _():
            s_wait(r, zl, 1)
            part[r, zl] = part[r, zl] + rbuf[1, r, zl].astype(F32)

        s_wait(r, zl, 2)
        out[r // 2, r % 2 * 128:r % 2 * 128 + 128] = (
            part[r, zl] + rbuf[2, r, zl].astype(F32)
        ).astype(BF16)

    prepare(0)
    bc_start(1)
    prepare(1)
    for i in (13, 1, 12):
        fetch(i).wait()
    bc_wait(0)
    ssd(0)
    g_start(0)
    spread(0, 0)
    spread(0, 1)
    bc_wait(1)
    ssd(1)
    z_copy(0).wait_send()
    z_copy(1).start()
    far_start(0)
    hand_over(zh, 0)
    hand_over(zh, 1)
    carry(0)
    for j in (1, 2, 3):
        g_copy(0, j).wait_send()
    g_start(1)
    spread(1, 0)
    carry(1)
    sib_all(zh)
    far_start(1)
    g_wait(0)
    project(0, zh)
    relay_all(0, zh)
    spread(1, 1)
    hand_over(1 - zh, 0)
    g_wait(1)
    project(1, zh)
    relay_all(1, zh)
    hand_over(1 - zh, 1)
    sib_all(1 - zh)
    project(0, 1 - zh)
    relay_all(0, 1 - zh)
    project(1, 1 - zh)
    relay_all(1, 1 - zh)
    for r in range(4):
        finish(r)

    for r in range(2):
        state_copy(r).wait()
    for b in range(2):
        for q in range(2):
            @pl.when(jnp.logical_not(a2a_local(b, q)))
            def _():
                for half in range(2):
                    for s in range(2):
                        a2a(half, s, b, q).wait_send()
    for s in range(2):
        if s == 1:
            z_copy(s).wait_send()
        for j in (1, 2, 3):
            y_copy(0, d_me, s, j).wait_send()
            y_copy(1, d_far, s, j).wait_send()
        for d in range(8):
            sib_copy(d, s).wait_send()
    for r in range(2):
        for j in (1, 2, 3):
            bc_copy(r, j).wait_send()
            if r == 1:
                g_copy(r, j).wait_send()
    for r in range(4):
        for d in range(8):
            @pl.when(d != zl)
            def _():
                s_copy(r, d, 0, d).wait_send()


def per_device(
    xs_in, gate_in, bc_in, dt_raw, x_tail, bc_tail, conv_x_w, conv_x_b, conv_bc_w, conv_bc_b,
    dt_bias, a_log, skip_d, state_in, norm_gain, out_values, out_scales,
):
    vmem = pl.BlockSpec(memory_space=pltpu.VMEM)
    stay = pl.BlockSpec(memory_space=pltpu.HBM)
    dma = pltpu.SemaphoreType.DMA
    operands = (
        xs_in.reshape(2, 256, 512), gate_in.reshape(2, 256, 512), bc_in.reshape(2, 256, 128),
        dt_raw.T, x_tail.transpose(1, 0, 2), bc_tail.transpose(1, 0, 2), conv_x_w,
        conv_x_b.reshape(1, 512), conv_bc_w, conv_bc_b.reshape(1, 128), dt_bias.reshape(1, 8),
        a_log.reshape(1, 8), skip_d.reshape(1, 8), state_in, norm_gain.reshape(1, 512),
        out_values, out_scales.T,
    )
    out, new_state = pl.pallas_call(
        kernel,
        name="mixer",
        out_shape=(
            jax.ShapeDtypeStruct((2, 256, 128), BF16),
            jax.ShapeDtypeStruct(state_in.shape, F32),
        ),
        in_specs=[stay] * 17,
        out_specs=(vmem, stay),
        scratch_shapes=[pltpu.VMEM(a.shape, a.dtype) for a in operands] + [
            pltpu.VMEM((2, 2, 2, 128, 128), BF16),
            pltpu.VMEM((2, 2, 2, 128, 128), BF16),
            pltpu.VMEM((8, 4, 4, 128, 128), BF16),
            pltpu.VMEM((4, 2, 256, 128), BF16),
            pltpu.VMEM((2, 4, 4, 256, 128), BF16),
            pltpu.VMEM((2, 4, 256, 128), BF16),
            pltpu.VMEM((264, 512), F32),
            pltpu.VMEM((264, 128), F32),
            pltpu.VMEM((2, 256, 128), F32),
            pltpu.VMEM((2, 256, 128), F32),
            pltpu.VMEM((2, 8, 256), F32),
            pltpu.VMEM((2, 8, 256), F32),
            pltpu.VMEM((256, 256), F32),
            pltpu.VMEM((4, 8, 128, 128), F32),
            pltpu.VMEM((4, 8, 128, 128), BF16),
            pltpu.VMEM((3, 4, 8, 128, 128), BF16),
            pltpu.VMEM((2, 8, 64, 256), F32),
            dma((17,)),
            dma((2,)),
            dma((2, 2, 2, 2)),
            dma((2, 2, 4)),
            dma((2, 2, 3)),
            dma((2,)),
            dma((2,)),
            dma((8, 2)),
            dma((8, 2)),
            dma((8, 2)),
            dma((2, 3)),
            dma((4, 2)),
            dma((2, 3)),
            dma((2, 4)),
            dma((4, 8)),
            dma((3, 4, 8)),
        ],
        compiler_params=pltpu.CompilerParams(
            collective_id=0, has_side_effects=True, vmem_limit_bytes=60 * 1024 * 1024
        ),
    )(*operands)
    return out.reshape(512, 128), new_state


def solution(mesh):
    placed = (
        P("fsdp", "chan"),
        P("fsdp", "chan"),
        P("fsdp", "chan"),
        P("fsdp", "chan"),
        P("fsdp", None, "chan"),
        P("fsdp", None, "chan"),
        P(None, "chan"),
        P("chan"),
        P(None, "chan"),
        P("chan"),
        P("chan"),
        P("chan"),
        P("chan"),
        P("fsdp", "chan", None, None),
        P("chan"),
        P("chan", "fsdp"),
        P("chan", "fsdp"),
    )
    return jax.shard_map(
        per_device,
        mesh=mesh,
        in_specs=placed,
        out_specs=(P("fsdp", "chan"), P("fsdp", "chan", None, None)),
        check_vma=False,
    )
```
